32 devices in a mesh: replica: 2 (over x), segment: 4 (over z), tensor: 4 (over y, core).
Axes of the slice: x: 2, y: 2, z: 4, core: 2. Of those that a mesh axis runs over, the one named last changes fastest.
Arguments:
- x_in: bfloat16 [256, 8192], P('replica', 'tensor'), parts along dimension 0, may hold values from -6 to 6
- norm_gain: float32 [4, 8192], P('segment'), may hold values from 0.5 to 1.5
- in_index: int32 [4, 224, 72], P('segment', 'tensor'), may hold values from -1 to 127, as said below
- gate_blocks: bfloat16 [4, 224, 72, 4096], P('segment', 'tensor'), may hold values from -0.09375 to 0.09375
- up_blocks: bfloat16 [4, 224, 72, 4096], P('segment', 'tensor'), may hold values from -0.09375 to 0.09375
- out_index: int32 [4, 128, 126], P('segment', 'tensor'), may hold values from -1 to 223, as said below
- down_blocks: bfloat16 [4, 128, 126, 4096], P('segment', 'tensor'), may hold values from -0.0625 to 0.0625
Outputs:
- sections: bfloat16 [4, 256, 8192], P('segment', 'replica', 'tensor'), parts along dimension 1
The draws below stay inside these ranges and needn't reach their ends.
There are 2 independent parts, one for each index of `replica`. The reference program is written for one: setup_inputs(seed, part) draws one part's arguments, and reference() takes and returns one part's arrays. A program takes and returns all parts, laid end to end along the dimension named above; an argument that names none is the same for every part. Nothing has to cross between parts.
Inputs may be any that keep to these rules, and one draw needn't show every extreme that they name: `in_index`: for each section and column block the entries name distinct row blocks, the kept ones first and -1 in the remaining slots; between 3 * 128 / 8 (rounded down) and 72 slots are kept, and in every section some column block keeps exactly 72 and another exactly the least. `out_index`: for each section and column block the entries name distinct row blocks, the kept ones first and -1 in the remaining slots; between 3 * 224 / 8 (rounded down) and 126 slots are kept, and in every section some column block keeps exactly 126 and another exactly the least.
All inputs are finite; a program needn't handle non-finite values.
Results may differ from the reference program's by a relative error of at most 0.0095.
Values may be sent and summed in bfloat16 or wider, within the bound.
A program may use at most 512 MiB of HBM per device.

```python
import jax
import jax.numpy as jnp
from jax import lax

D = 8192
FFW = 14336
BS = 64
TOKENS = 128
SEGMENTS = 4
RB_IN = 128
RB_OUT = 224
MAXB = 72
MAXO = 126


def mask_lists(key, tile_count, row_blocks, most_kept):
    least_kept = 3 * row_blocks // 8
    key_perm, key_count, key_highest, key_lowest = jax.random.split(key, 4)
    key_list = jax.random.split(key_perm, SEGMENTS * tile_count)

    def one_order(single_key):
        return jax.random.permutation(single_key, row_blocks)
    orders = jax.vmap(one_order)(key_list)[:, :most_kept]
    orders = orders.reshape(SEGMENTS, tile_count, most_kept).astype(jnp.int32)
    counts = jax.random.randint(key_count, (SEGMENTS, tile_count), least_kept, most_kept + 1)
    highest = jax.random.randint(key_highest, (SEGMENTS, 1), 0, tile_count)
    lowest = (highest + 1 + jax.random.randint(key_lowest, (SEGMENTS, 1), 0, tile_count - 1)) % tile_count
    column = jnp.arange(tile_count)[None, :]
    counts = jnp.where(column == highest, most_kept, counts)
    counts = jnp.where(column == lowest, least_kept, counts)
    slot_ids = jnp.arange(most_kept)[None, None, :]
    return jnp.where(slot_ids < counts[:, :, None], orders, -1).astype(jnp.int32)


def draw_in_index(key, part):
    return mask_lists(jax.random.fold_in(key, 11), RB_OUT, RB_IN, MAXB)


def draw_out_index(key, part):
    return mask_lists(jax.random.fold_in(key, 12), RB_IN, RB_OUT, MAXO)


def level_of(rng, shape, cuts, smallest, top_value):
    loudness, own = 1.0, jax.random.fold_in(rng, 6)
    for axis_at, blocks in cuts:
        draws = jnp.exp(jax.random.uniform(jax.random.fold_in(own, axis_at), (blocks,), jnp.float32, smallest / len(cuts), top_value / len(cuts)))
        loudness = loudness * jnp.repeat(draws, shape[axis_at] // blocks).reshape([-1 if axis == axis_at else 1 for axis in range(len(shape))])
    return loudness


def centred(own_key, shape, width, limit, pieces=(), held_as=jnp.bfloat16):
    loudness = level_of(own_key, shape, pieces, -0.22, 0.18) if pieces else 1.0
    array = jax.random.normal(own_key, shape, jnp.float32) * width * loudness
    return jnp.minimum(jnp.maximum(array, -limit), limit).astype(held_as)


def setup_inputs(seed: int = 0, part: int = 0) -> dict:
    streams_of = jax.random.split(jax.random.key(seed), 8)
    part_keys = jax.random.split(jax.random.fold_in(streams_of[7], part), 8)
    return {
        "x_in": centred(part_keys[0], (TOKENS, D), 1.0, 6.0, ((1, 4),)),
        "norm_gain": jnp.clip(1.0 + 0.1 * jax.random.normal(streams_of[1], (SEGMENTS, D), jnp.float32), 0.5, 1.5),
        "in_index": draw_in_index(jax.random.fold_in(streams_of[7], 71), part),
        "gate_blocks": centred(streams_of[3], (SEGMENTS, RB_OUT, MAXB, BS * BS), (D // 2) ** -0.5, 0.09375, ((0, 4), (1, 4))),
        "up_blocks": centred(streams_of[4], (SEGMENTS, RB_OUT, MAXB, BS * BS), (D // 2) ** -0.5, 0.09375, ((0, 4), (1, 4))),
        "out_index": draw_out_index(jax.random.fold_in(streams_of[7], 71), part),
        "down_blocks": centred(streams_of[6], (SEGMENTS, RB_IN, MAXO, BS * BS), (FFW // 2) ** -0.5, 0.0625, ((0, 4), (1, 4))),
    }


def sparse_apply(left, index, blocks):
    rows = left.shape[0]
    split_rows = left.reshape(rows, -1, BS).astype(jnp.float32)

    def one_tile(pair):
        tile_index, tile_blocks = pair
        kept = (tile_index >= 0).astype(jnp.float32)
        safe_index = jnp.maximum(tile_index, 0).astype(jnp.int32)
        taken = jnp.take(split_rows, safe_index, axis=1)
        weights = tile_blocks.astype(jnp.float32).reshape(-1, BS, BS) * kept[:, None, None]
        return jnp.einsum('rmi,mij->rj', taken, weights)
    tiles = lax.map(one_tile, (index, blocks))
    return jnp.transpose(tiles, (1, 0, 2)).reshape(rows, -1)

def reference(x_in, norm_gain, in_index, gate_blocks, up_blocks, out_index, down_blocks):
    current = x_in
    results = []
    for section in range(SEGMENTS):
        wide = current.astype(jnp.float32)
        stat = lax.optimization_barrier(jnp.mean(wide * wide, axis=1, keepdims=True))
        normed = (wide * lax.rsqrt(stat + 1e-05) * norm_gain[section][None, :]).astype(jnp.bfloat16)
        gate = sparse_apply(normed, in_index[section], gate_blocks[section])
        up_part = sparse_apply(normed, in_index[section], up_blocks[section])
        hidden = (jax.nn.silu(gate) * up_part).astype(jnp.bfloat16)
        mixed = sparse_apply(hidden, out_index[section], down_blocks[section])
        current = (wide + mixed).astype(jnp.bfloat16)
        results.append(current)
    return jnp.stack(results)
```

```python
import jax
import jax.numpy as jnp
from jax import lax
from jax.experimental import pallas as pl
from jax.experimental.pallas import tpu as pltpu
from jax.sharding import PartitionSpec as P

BS = 64
LANES = 2 * BS
VMEM_LIMIT = 56 * 1024 * 1024


def swap_halves(value):
    return jnp.concatenate([value[:, BS:], value[:, :BS]], axis=1)


def picks_of(index_row, row_blocks):
    slots = index_row.shape[1]
    rows = lax.broadcasted_iota(jnp.int32, (row_blocks, slots), 0)
    return (index_row == rows).astype(jnp.float32).astype(jnp.bfloat16)


def expand_in_kernel(row_blocks, index_ref, gate_ref, up_ref, out_ref):
    picks = picks_of(index_ref[0], row_blocks)
    slots = gate_ref.shape[1]
    low = lax.broadcasted_iota(jnp.int32, (slots, LANES), 1) < BS
    for pair in range(BS // 2):
        gate = gate_ref[0, :, pair * LANES : (pair + 1) * LANES]
        up = up_ref[0, :, pair * LANES : (pair + 1) * LANES]
        both = jnp.concatenate(
            [jnp.where(low, gate, swap_halves(up)), jnp.where(low, swap_halves(gate), up)], axis=1
        )
        dense = jnp.dot(picks, both, preferred_element_type=jnp.float32).astype(jnp.bfloat16)
        at = 2 * pair * row_blocks
        out_ref[at : at + row_blocks, :] = dense[:, :LANES]
        out_ref[at + row_blocks : at + 2 * row_blocks, :] = dense[:, LANES:]


def expand_in(index, gate_blocks, up_blocks, row_blocks):
    tiles, slots, size = gate_blocks.shape
    padded = tiles + tiles % 2
    return pl.pallas_call(
        lambda *refs: expand_in_kernel(row_blocks, *refs),
        grid=(tiles,),
        in_specs=[
            pl.BlockSpec((1, 1, slots), lambda c: (c, 0, 0)),
            pl.BlockSpec((1, slots, size), lambda c: (c, 0, 0)),
            pl.BlockSpec((1, slots, size), lambda c: (c, 0, 0)),
        ],
        out_specs=pl.BlockSpec((row_blocks * BS, LANES), lambda c: (0, c)),
        out_shape=jax.ShapeDtypeStruct((row_blocks * BS, padded * LANES), jnp.bfloat16),
        compiler_params=pltpu.CompilerParams(vmem_limit_bytes=VMEM_LIMIT),
        name="expand_in",
    )(index[:, None, :], gate_blocks, up_blocks)


def expand_out_kernel(row_blocks, index_ref, blocks_ref, out_ref):
    first = picks_of(index_ref[0, 0:1, :], row_blocks)
    second = picks_of(index_ref[0, 1:2, :], row_blocks)
    low = lax.broadcasted_iota(jnp.int32, (row_blocks, LANES), 1) < BS
    for quad in range(BS // 4):
        cols = slice(quad * 2 * LANES, (quad + 1) * 2 * LANES)
        left = jnp.dot(first, blocks_ref[0, :, cols], preferred_element_type=jnp.float32)
        right = jnp.dot(second, blocks_ref[1, :, cols], preferred_element_type=jnp.float32)
        for half in range(2):
            a = left[:, half * LANES : (half + 1) * LANES]
            b = right[:, half * LANES : (half + 1) * LANES]
            at = (4 * quad + 2 * half) * row_blocks
            out_ref[at : at + row_blocks, :] = jnp.where(low, a, pltpu.roll(b, BS, 1)).astype(jnp.bfloat16)
            out_ref[at + row_blocks : at + 2 * row_blocks, :] = jnp.where(
                low, pltpu.roll(a, BS, 1), b
            ).astype(jnp.bfloat16)


def expand_out(index, blocks, row_blocks):
    tiles, slots, size = blocks.shape
    return pl.pallas_call(
        lambda *refs: expand_out_kernel(row_blocks, *refs),
        grid=(tiles // 2,),
        in_specs=[
            pl.BlockSpec((1, 2, slots), lambda c: (c, 0, 0)),
            pl.BlockSpec((2, slots, size), lambda c: (c, 0, 0)),
        ],
        out_specs=pl.BlockSpec((row_blocks * BS, LANES), lambda c: (0, c)),
        out_shape=jax.ShapeDtypeStruct((row_blocks * BS, tiles * BS), jnp.bfloat16),
        compiler_params=pltpu.CompilerParams(vmem_limit_bytes=VMEM_LIMIT),
        name="expand_out",
    )(index.reshape(tiles // 2, 2, slots), blocks)


def gate_up_kernel(x_ref, w_ref, out_ref):
    both = jnp.dot(x_ref[...], w_ref[...], preferred_element_type=jnp.float32)
    a, b = both[:, :LANES], both[:, LANES:]
    low = lax.broadcasted_iota(jnp.int32, a.shape, 1) < BS
    gate = jnp.where(low, a, pltpu.roll(b, BS, 1))
    up = jnp.where(low, pltpu.roll(a, BS, 1), b)
    out_ref[...] = (gate / (1.0 + jnp.exp(-gate)) * up).astype(jnp.bfloat16)


def gate_up(x, weights):
    rows, depth = x.shape
    steps = weights.shape[1] // (2 * LANES)
    return pl.pallas_call(
        gate_up_kernel,
        grid=(steps,),
        in_specs=[
            pl.BlockSpec((rows, depth), lambda n: (0, 0)),
            pl.BlockSpec((depth, 2 * LANES), lambda n: (0, n)),
        ],
        out_specs=pl.BlockSpec((rows, LANES), lambda n: (0, n)),
        out_shape=jax.ShapeDtypeStruct((rows, steps * LANES), jnp.bfloat16),
        compiler_params=pltpu.CompilerParams(vmem_limit_bytes=VMEM_LIMIT),
        name="gate_up",
    )(x, weights)


def down_kernel(h_ref, w_ref, x_ref, out_ref):
    mixed = jnp.dot(h_ref[...], w_ref[...], preferred_element_type=jnp.float32)
    out_ref[...] = (x_ref[...].astype(jnp.float32) + mixed).astype(jnp.bfloat16)


def down(hidden, weights, x):
    rows, depth = hidden.shape
    cols = weights.shape[1]
    width = 2 * LANES if cols % (2 * LANES) == 0 else LANES
    return pl.pallas_call(
        down_kernel,
        grid=(cols // width,),
        in_specs=[
            pl.BlockSpec((rows, depth), lambda n: (0, 0)),
            pl.BlockSpec((depth, width), lambda n: (0, n)),
            pl.BlockSpec((rows, width), lambda n: (0, n)),
        ],
        out_specs=pl.BlockSpec((rows, width), lambda n: (0, n)),
        out_shape=jax.ShapeDtypeStruct((rows, cols), jnp.bfloat16),
        compiler_params=pltpu.CompilerParams(vmem_limit_bytes=VMEM_LIMIT),
        name="down",
    )(hidden, weights, x)


def by_inner_row(value):
    rows, cols = value.shape
    return value.reshape(rows, cols // BS, BS).swapaxes(1, 2).reshape(rows, cols)


def local(x_in, norm_gain, in_index, gate_blocks, up_blocks, out_index, down_blocks):
    segment_count = lax.axis_size("segment")
    tensor_count = lax.axis_size("tensor")
    segment_at = lax.axis_index("segment")
    gain_row = norm_gain[0]
    local_hidden = in_index.shape[1] * BS
    weights_in = expand_in(in_index[0], gate_blocks[0], up_blocks[0], gain_row.shape[0] // BS)
    weights_out = expand_out(out_index[0], down_blocks[0], tensor_count * local_hidden // BS)
    pairs = [(i, i + 1) for i in range(segment_count - 1)]
    incoming = x_in
    result = jnp.zeros_like(x_in)
    for tick in range(segment_count):
        whole = lax.all_gather(incoming, "tensor", axis=1, tiled=True)
        wide = whole.astype(jnp.float32)
        stat = jnp.mean(wide * wide, axis=1, keepdims=True)
        normed = (wide * lax.rsqrt(stat + 1e-05) * gain_row[None, :]).astype(jnp.bfloat16)
        hidden = gate_up(by_inner_row(normed), weights_in)[:, :local_hidden]
        hidden = lax.all_gather(hidden, "tensor", axis=1, tiled=True)
        produced = down(by_inner_row(hidden), weights_out, incoming)
        result = jnp.where(segment_at == tick, produced, result)
        if tick + 1 < segment_count:
            incoming = lax.ppermute(produced, "segment", pairs)
    return result[None]


def solution(mesh):
    placed = (
        P("replica", "tensor"),
        P("segment", None),
        P("segment", "tensor", None),
        P("segment", "tensor", None, None),
        P("segment", "tensor", None, None),
        P("segment", "tensor", None),
        P("segment", "tensor", None, None),
    )
    return jax.shard_map(
        local,
        mesh=mesh,
        in_specs=placed,
        out_specs=P("segment", "replica", "tensor"),
        check_vma=False,
    )
```

```python
import math

import jax
import jax.numpy as jnp
from jax import lax
from jax.experimental import pallas as pl
from jax.experimental.pallas import tpu as pltpu
from jax.sharding import PartitionSpec as P

BS = 64
LANES = 2 * BS
VMEM_LIMIT = 56 * 1024 * 1024


def swap_halves(value):
    return jnp.concatenate([value[:, BS:], value[:, :BS]], axis=1)


def picks_of(index_row, row_blocks):
    slots = index_row.shape[1]
    rows = lax.broadcasted_iota(jnp.int32, (row_blocks, slots), 0)
    return (index_row == rows).astype(jnp.float32).astype(jnp.bfloat16)


def store_rows(even, odd, pair, groups, out_ref):
    base = 0
    for first, count in groups:
        rows = jnp.concatenate([even[first : first + count], odd[first : first + count]], axis=0)
        at = base + 2 * pair * count
        out_ref[at : at + 2 * count, :] = rows.astype(jnp.bfloat16)
        base += BS * count


def expand_in_kernel(row_blocks, groups, index_ref, gate_ref, up_ref, out_ref):
    picks = picks_of(index_ref[0], row_blocks)
    slots = gate_ref.shape[1]
    low = lax.broadcasted_iota(jnp.int32, (slots, LANES), 1) < BS
    for pair in range(BS // 2):
        gate = gate_ref[0, :, pair * LANES : (pair + 1) * LANES]
        up = up_ref[0, :, pair * LANES : (pair + 1) * LANES]
        both = jnp.concatenate(
            [jnp.where(low, gate, swap_halves(up)), jnp.where(low, swap_halves(gate), up)], axis=1
        )
        dense = jnp.dot(picks, both, preferred_element_type=jnp.float32)
        store_rows(dense[:, :LANES], dense[:, LANES:], pair, groups, out_ref)


def cost(flops, *arrays):
    moved = sum(math.prod(a.shape) * a.dtype.itemsize for a in arrays)
    return pl.CostEstimate(flops=flops, bytes_accessed=moved, transcendentals=0)


def expand_in(index, gate_blocks, up_blocks, row_blocks, groups):
    tiles, slots, size = gate_blocks.shape
    padded = tiles + tiles % 2
    shape = jax.ShapeDtypeStruct((row_blocks * BS, padded * LANES), jnp.bfloat16)
    return pl.pallas_call(
        lambda *refs: expand_in_kernel(row_blocks, groups, *refs),
        grid=(tiles,),
        in_specs=[
            pl.BlockSpec((1, 1, slots), lambda c: (c, 0, 0)),
            pl.BlockSpec((1, slots, size), lambda c: (c, 0, 0)),
            pl.BlockSpec((1, slots, size), lambda c: (c, 0, 0)),
        ],
        out_specs=pl.BlockSpec((row_blocks * BS, LANES), lambda c: (0, c)),
        out_shape=shape,
        compiler_params=pltpu.CompilerParams(vmem_limit_bytes=VMEM_LIMIT),
        cost_estimate=cost(0, gate_blocks, up_blocks, shape),
        name="expand_in",
    )(index[:, None, :], gate_blocks, up_blocks)


def expand_out_kernel(row_blocks, chunks, index_ref, blocks_ref, *out_refs):
    first = picks_of(index_ref[0, 0:1, :], row_blocks)
    second = picks_of(index_ref[0, 1:2, :], row_blocks)
    low = lax.broadcasted_iota(jnp.int32, (row_blocks, LANES), 1) < BS
    for quad in range(BS // 4):
        cols = slice(quad * 2 * LANES, (quad + 1) * 2 * LANES)
        left = jnp.dot(first, blocks_ref[0, :, cols], preferred_element_type=jnp.float32)
        right = jnp.dot(second, blocks_ref[1, :, cols], preferred_element_type=jnp.float32)
        for half in range(2):
            a = left[:, half * LANES : (half + 1) * LANES]
            b = right[:, half * LANES : (half + 1) * LANES]
            even = jnp.where(low, a, pltpu.roll(b, BS, 1))
            odd = jnp.where(low, pltpu.roll(a, BS, 1), b)
            for groups, out_ref in zip(chunks, out_refs):
                store_rows(even, odd, 2 * quad + half, groups, out_ref)


def expand_out(index, blocks, row_blocks, chunks):
    tiles, slots, size = blocks.shape
    depths = [BS * sum(count for _, count in groups) for groups in chunks]
    shapes = [jax.ShapeDtypeStruct((depth, tiles * BS), jnp.bfloat16) for depth in depths]
    return pl.pallas_call(
        lambda *refs: expand_out_kernel(row_blocks, chunks, *refs),
        grid=(tiles // 2,),
        in_specs=[
            pl.BlockSpec((1, 2, slots), lambda c: (c, 0, 0)),
            pl.BlockSpec((2, slots, size), lambda c: (c, 0, 0)),
        ],
        out_specs=[pl.BlockSpec((depth, LANES), lambda c: (0, c)) for depth in depths],
        out_shape=shapes,
        compiler_params=pltpu.CompilerParams(vmem_limit_bytes=VMEM_LIMIT),
        cost_estimate=cost(0, blocks, *shapes),
        name="expand_out",
    )(index.reshape(tiles // 2, 2, slots), blocks)


def gate_up_kernel(x_ref, w_ref, out_ref):
    both = jnp.dot(x_ref[...], w_ref[...], preferred_element_type=jnp.float32)
    a, b = both[:, :LANES], both[:, LANES:]
    low = lax.broadcasted_iota(jnp.int32, a.shape, 1) < BS
    gate = jnp.where(low, a, pltpu.roll(b, BS, 1))
    up = jnp.where(low, pltpu.roll(a, BS, 1), b)
    out_ref[...] = (gate / (1.0 + jnp.exp(-gate)) * up).astype(jnp.bfloat16)


def gate_up(x, weights, first, steps):
    rows, depth = x.shape
    shape = jax.ShapeDtypeStruct((rows, steps * LANES), jnp.bfloat16)
    used = jax.ShapeDtypeStruct((depth, steps * 2 * LANES), jnp.bfloat16)
    return pl.pallas_call(
        gate_up_kernel,
        grid=(steps,),
        in_specs=[
            pl.BlockSpec((rows, depth), lambda n: (0, 0)),
            pl.BlockSpec((depth, 2 * LANES), lambda n: (0, n + first)),
        ],
        out_specs=pl.BlockSpec((rows, LANES), lambda n: (0, n)),
        out_shape=shape,
        compiler_params=pltpu.CompilerParams(vmem_limit_bytes=VMEM_LIMIT),
        cost_estimate=cost(2 * rows * depth * steps * 2 * LANES, x, used, shape),
        name="gate_up",
    )(x, weights)


def down_kernel(h_ref, w_ref, total_ref, out_ref):
    mixed = jnp.dot(h_ref[...], w_ref[...], preferred_element_type=jnp.float32)
    out_ref[...] = (total_ref[...].astype(jnp.float32) + mixed).astype(out_ref.dtype)


def down(hidden, weights, total, dtype):
    rows, depth = hidden.shape
    cols = weights.shape[1]
    width = 2 * LANES if cols % (2 * LANES) == 0 else LANES
    shape = jax.ShapeDtypeStruct((rows, cols), dtype)
    return pl.pallas_call(
        down_kernel,
        grid=(cols // width,),
        in_specs=[
            pl.BlockSpec((rows, depth), lambda n: (0, 0)),
            pl.BlockSpec((depth, width), lambda n: (0, n)),
            pl.BlockSpec((rows, width), lambda n: (0, n)),
        ],
        out_specs=pl.BlockSpec((rows, width), lambda n: (0, n)),
        out_shape=shape,
        compiler_params=pltpu.CompilerParams(vmem_limit_bytes=VMEM_LIMIT),
        cost_estimate=cost(2 * rows * depth * cols, hidden, weights, total, shape),
        name="down",
    )(hidden, weights, total)


def by_inner_row(value, groups=1):
    rows, cols = value.shape
    split = value.reshape(rows, groups, cols // (groups * BS), BS)
    return split.swapaxes(2, 3).reshape(rows, cols)


def gathered(value, split):
    if split:
        return lax.all_gather(by_inner_row(value), "tensor", axis=1, tiled=True)
    return by_inner_row(lax.all_gather(value, "tensor", axis=1, tiled=True))


def local(x_in, norm_gain, in_index, gate_blocks, up_blocks, out_index, down_blocks):
    segment_count = lax.axis_size("segment")
    devices = lax.axis_size("tensor")
    segment_at = lax.axis_index("segment")
    gain_row = norm_gain[0]
    tiles = in_index.shape[1]
    in_blocks = gain_row.shape[0] // BS
    per_device = in_blocks // devices
    split_in = per_device % 8 == 0
    groups_in = [(d * per_device, per_device) for d in range(devices)] if split_in else [(0, in_blocks)]
    gain_row = by_inner_row(gain_row[None, :], len(groups_in))
    split_out = tiles % 8 == 0
    if split_out:
        early = -(-tiles // 16) * 8
        parts = [(0, early), (early, tiles - early)] if early < tiles else [(0, tiles)]
        chunks = [[(d * tiles + at, count) for d in range(devices)] for at, count in parts]
    else:
        parts = [(0, tiles)]
        chunks = [[(0, devices * tiles)]]
    weights_in = expand_in(in_index[0], gate_blocks[0], up_blocks[0], in_blocks, groups_in)
    weights_out = expand_out(out_index[0], down_blocks[0], devices * tiles, chunks)
    pairs = [(i, i + 1) for i in range(segment_count - 1)]
    incoming = x_in
    result = jnp.zeros_like(x_in)
    for tick in range(segment_count):
        wide = gathered(incoming, split_in).astype(jnp.float32)
        stat = jnp.mean(wide * wide, axis=1, keepdims=True)
        normed = (wide * lax.rsqrt(stat + 1e-05) * gain_row).astype(jnp.bfloat16)
        hidden = []
        for at, count in parts:
            part = gate_up(normed, weights_in, at // 2, -(-count // 2))[:, : count * BS]
            hidden.append(gathered(part, split_out))
        total = incoming
        for order, (part, weights) in enumerate(zip(hidden, weights_out)):
            last = order + 1 == len(hidden)
            total = down(part, weights, total, jnp.bfloat16 if last else jnp.float32)
        result = jnp.where(segment_at == tick, total, result)
        if tick + 1 < segment_count:
            incoming = lax.ppermute(total, "segment", pairs)
    return result[None]


def solution(mesh):
    placed = (
        P("replica", "tensor"),
        P("segment", None),
        P("segment", "tensor", None),
        P("segment", "tensor", None, None),
        P("segment", "tensor", None, None),
        P("segment", "tensor", None),
        P("segment", "tensor", None, None),
    )
    return jax.shard_map(
        local,
        mesh=mesh,
        in_specs=placed,
        out_specs=P("segment", "replica", "tensor"),
        check_vma=False,
    )
```
